32 devices in a mesh: groups: 2 (over y), seq: 4 (over x, core), dp: 4 (over z).
Axes of the slice: x: 2, y: 2, z: 4, core: 2. Of those that a mesh axis runs over, the one named last changes fastest.
Arguments:
- hidden_states: bfloat16 [8, 8, 256, 1152], P(('groups', 'dp'), 'seq'), parts along dimension 0, may hold values from -80 to 80
- modulation: float32 [8, 3, 1152], P(('groups', 'dp')), parts along dimension 0, may hold values from -0.5 to 1
- qkv_weight: bfloat16 [1152, 1728], P('dp'), may hold values from -0.1875 to 0.1875
- qk_gain: float32 [2, 72], replicated, may hold values from 0.5 to 4
- out_weight: bfloat16 [576, 1152], replicated, may hold values from -0.25 to 0.25
- out_cotangent: bfloat16 [8, 8, 256, 1152], P(('groups', 'dp'), 'seq'), parts along dimension 0, may hold values from -6 to 6
Outputs:
- grad_hidden: bfloat16 [8, 8, 256, 1152], P(('groups', 'dp'), 'seq'), parts along dimension 0
- grad_out_weight: float32 [1152, 1152], P(('groups', 'seq'), 'dp'), parts along dimension 0
The draws below stay inside these ranges and needn't reach their ends.
There are 2 independent parts, one for each index of `groups`. The reference program is written for one: setup_inputs(seed, part) draws one part's arguments, and reference() takes and returns one part's arrays. A program takes and returns all parts, laid end to end along the dimension named above; an argument that names none is the same for every part. Nothing has to cross between parts.
All inputs are finite; a program needn't handle non-finite values.
Results may differ from the reference program's by a relative error of at most 0.012.
The reference program's roundings to bfloat16 on the way count: a program that leaves them out, or rounds other values in their place, can miss the bound.
Values may be sent and summed in bfloat16 or wider, within the bound.
A program may use at most 64 MiB of HBM per device.

```python
import math
import jax
import jax.numpy as jnp
from jax import lax

D = 1152
HEADS = 8
HD = 72
S = 256
FRAMES = 8
VIDEOS = 4


def draw_hidden_states(key, part):
    key = jax.random.fold_in(key, 11)
    key_base, key_rows, key_cols = jax.random.split(key, 3)
    shape = (VIDEOS, FRAMES, S, D)
    row_scale = jnp.exp(jax.random.uniform(key_rows, (VIDEOS, FRAMES, S, 1), jnp.float32, math.log(0.5), math.log(5.0)))
    col_scale = jnp.exp(jax.random.uniform(key_cols, (VIDEOS, 1, 1, D), jnp.float32, math.log(0.5), math.log(2.5)))
    base = jnp.clip(jax.random.normal(key_base, shape, jnp.float32), -6.0, 6.0)
    return (base * row_scale * col_scale).astype(jnp.bfloat16)


def draw_qk_gain(key, part):
    key = jax.random.fold_in(key, 23)
    lower, upper = (0.5, 1.6)
    return jnp.exp(jax.random.uniform(key, (2, HD), jnp.float32, math.log(lower), math.log(upper)))


def level_of(own_key, shape, cuts, smallest, top_value):
    def one(position, shards_of):
        heights = jax.random.uniform(jax.random.fold_in(jax.random.fold_in(own_key, 6), position), (shards_of,), jnp.float32, smallest / len(cuts), top_value / len(cuts))
        return jnp.repeat(jnp.exp(heights), shape[position] // shards_of).reshape((-1,) + (1,) * (len(shape) - position - 1))

    loudness = one(*cuts[0])
    for cut in cuts[1:]:
        loudness = loudness * one(*cut)
    return loudness


def centred(rng, extent, width, most, pieces=(), held_as=jnp.bfloat16):
    loudness = level_of(rng, extent, pieces, -0.22, 0.18) if pieces else 1.0
    entries = jax.random.normal(rng, extent, jnp.float32) * width * loudness
    return jnp.minimum(jnp.maximum(entries, -most), most).astype(held_as)


def setup_inputs(seed: int = 0, part: int = 0) -> dict:
    keys = jax.random.split(jax.random.key(seed), 7)
    part_splits = jax.random.split(jax.random.fold_in(keys[6], part), 7)
    return {
        "hidden_states": draw_hidden_states(jax.random.fold_in(jax.random.fold_in(keys[6], part), 71), part),
        "modulation": jnp.clip(-0.5 + 1.5 * jax.random.uniform(part_splits[1], (VIDEOS, 3, D), jnp.float32) ** level_of(part_splits[1], (VIDEOS, 3, D), ((0, 4),), -0.2, 0.2), -0.5, 1.0),
        "qkv_weight": centred(keys[2], (D, 3 * HEADS * HD), D ** -0.5, 0.1875, ((0, 4),)),
        "qk_gain": draw_qk_gain(jax.random.fold_in(keys[6], 71), part),
        "out_weight": centred(keys[4], (HEADS * HD, D), (HEADS * HD) ** -0.5, 0.25),
        "out_cotangent": centred(part_splits[5], (VIDEOS, FRAMES, S, D), 1.0, 6.0, ((0, 4), (1, 4))),
    }


norm_eps = 1e-06

def layer_normed(values):
    centered = values - lax.optimization_barrier(jnp.mean(values, -1, keepdims=True))
    inverse = lax.rsqrt(lax.optimization_barrier(jnp.mean(centered * centered, -1, keepdims=True)) + norm_eps)
    return (centered * inverse, inverse)

def rms_normed(values, gain_row):
    inverse = lax.rsqrt(lax.optimization_barrier(jnp.mean(values * values, -1, keepdims=True)) + norm_eps)
    return (values * inverse * gain_row, inverse)

def rms_back(values, inverse, gain_row, grad_out):
    scaled = grad_out * gain_row
    return inverse * scaled - values * inverse * inverse * inverse * lax.optimization_barrier(jnp.mean(values * scaled, -1, keepdims=True))

def temporal_forward(packed, qk_gain):
    frames, tokens = (packed.shape[0], packed.shape[1])
    score_scale = HD ** (-0.5)
    unpacked = packed.reshape(frames, tokens, 3, HEADS, HD)
    queries = unpacked[:, :, 0].astype(jnp.float32)
    keys_raw = unpacked[:, :, 1].astype(jnp.float32)
    values = unpacked[:, :, 2]
    query_n, query_inv = rms_normed(queries, qk_gain[0])
    key_n, key_inv = rms_normed(keys_raw, qk_gain[1])
    query_b = query_n.astype(jnp.bfloat16)
    key_b = key_n.astype(jnp.bfloat16)
    scores = jnp.einsum('fshd,gshd->shfg', query_b.astype(jnp.float32), key_b.astype(jnp.float32), precision=lax.Precision.HIGHEST) * score_scale
    shifted = jnp.exp(scores - lax.optimization_barrier(jnp.max(scores, -1, keepdims=True)))
    softmax_probs = shifted / lax.optimization_barrier(jnp.sum(shifted, -1, keepdims=True))
    probs_b = softmax_probs.astype(jnp.bfloat16)
    attended = jnp.einsum('shfg,gshd->fshd', probs_b.astype(jnp.float32), values.astype(jnp.float32), precision=lax.Precision.HIGHEST).astype(jnp.bfloat16)
    stored = (queries, keys_raw, values, query_inv, key_inv, query_b, key_b, softmax_probs, probs_b)
    return (attended.reshape(frames, tokens, HEADS * HD), stored)

def temporal_backward(stored, qk_gain, grad_att):
    queries, keys_raw, values, query_inv, key_inv, query_b, key_b, softmax_probs, probs_b = stored
    frames, tokens = (queries.shape[0], queries.shape[1])
    score_scale = HD ** (-0.5)
    grad_heads = grad_att.reshape(frames, tokens, HEADS, HD).astype(jnp.float32)
    grad_values = jnp.einsum('shfg,fshd->gshd', probs_b.astype(jnp.float32), grad_heads, precision=lax.Precision.HIGHEST)
    grad_probs = jnp.einsum('fshd,gshd->shfg', grad_heads, values.astype(jnp.float32), precision=lax.Precision.HIGHEST)
    grad_scores = softmax_probs * (grad_probs - lax.optimization_barrier(jnp.sum(softmax_probs * grad_probs, -1, keepdims=True))) * score_scale
    grad_qn = jnp.einsum('shfg,gshd->fshd', grad_scores, key_b.astype(jnp.float32), precision=lax.Precision.HIGHEST)
    grad_kn = jnp.einsum('shfg,fshd->gshd', grad_scores, query_b.astype(jnp.float32), precision=lax.Precision.HIGHEST)
    grad_query = rms_back(queries, query_inv, qk_gain[0], grad_qn)
    grad_keys = rms_back(keys_raw, key_inv, qk_gain[1], grad_kn)
    stacked = jnp.stack([grad_query, grad_keys, grad_values], axis=2).astype(jnp.bfloat16)
    return stacked.reshape(frames, tokens, 3 * HEADS * HD)

def one_video(states, modulation_row, cotangent, qkv_weight, qk_gain, out_weight):
    frames, tokens, features = states.shape
    normed, inverse = layer_normed(states.astype(jnp.float32))
    modulated = (normed * (1.0 + modulation_row[1]) + modulation_row[0]).astype(jnp.bfloat16)
    packed = jnp.dot(modulated.reshape(-1, features), qkv_weight, preferred_element_type=jnp.float32).astype(jnp.bfloat16).reshape(frames, tokens, -1)
    attended, stored = temporal_forward(packed, qk_gain)
    gated = (modulation_row[2] * cotangent.astype(jnp.float32)).astype(jnp.bfloat16)
    flat_att = attended.reshape(-1, attended.shape[-1])
    flat_gated = gated.reshape(-1, features)
    weight_term = lax.dot_general(flat_att, flat_gated, (((0,), (0,)), ((), ())), preferred_element_type=jnp.float32)
    grad_att = lax.dot_general(flat_gated, out_weight, (((1,), (1,)), ((), ())), preferred_element_type=jnp.float32).astype(jnp.bfloat16)
    grad_packed = temporal_backward(stored, qk_gain, grad_att.reshape(frames, tokens, -1))
    grad_mod = lax.dot_general(grad_packed.reshape(-1, grad_packed.shape[-1]), qkv_weight, (((1,), (1,)), ((), ())), preferred_element_type=jnp.float32).astype(jnp.bfloat16).reshape(frames, tokens, features)
    grad_normed = grad_mod.astype(jnp.float32) * (1.0 + modulation_row[1])
    grad_ln = inverse * (grad_normed - lax.optimization_barrier(jnp.mean(grad_normed, -1, keepdims=True)) - normed * lax.optimization_barrier(jnp.mean(grad_normed * normed, -1, keepdims=True)))
    grad_states = (cotangent.astype(jnp.float32) + grad_ln).astype(jnp.bfloat16)
    return (grad_states, weight_term)

def reference(hidden_states, modulation, qkv_weight, qk_gain, out_weight, out_cotangent):

    def per_video(video_items):
        return one_video(video_items[0], video_items[1], video_items[2], qkv_weight, qk_gain, out_weight)
    grad_hidden, weight_terms = lax.map(per_video, (hidden_states, modulation, out_cotangent))
    return (grad_hidden, lax.optimization_barrier(jnp.sum(weight_terms, axis=0)))
```

```python
import functools

import jax
import jax.numpy as jnp
import numpy as np
from jax import lax
from jax.experimental import pallas as pl
from jax.experimental.pallas import tpu as pltpu
from jax.sharding import PartitionSpec as P

HEADS = 8
HD = 72
WIDE = HEADS * HD
LANES = 128
PAD = -(-WIDE // LANES) * LANES
EPS = 1e-06
MESH = pl.DeviceIdType.MESH
F32 = jnp.float32
BF16 = jnp.bfloat16


def head_tiles(head):
    return range(head * HD // LANES, (head * HD + HD - 1) // LANES + 1)


def dot_nn(a, b):
    return lax.dot_general(a, b, (((1,), (0,)), ((), ())), preferred_element_type=F32)


def dot_nt(a, b):
    return lax.dot_general(a, b, (((1,), (1,)), ((), ())), preferred_element_type=F32)


def dot_tn(a, b):
    return lax.dot_general(a, b, (((0,), (0,)), ((), ())), preferred_element_type=F32)


def head_sum(values, ones):
    high = values.astype(BF16)
    low = (values - high.astype(F32)).astype(BF16)
    return dot_nn(high, ones) + dot_nn(low, ones)


def head_window(array, head, masked):
    tiles = head_tiles(head)
    low = tiles[0] * LANES
    window = array[:, low : low + len(tiles) * LANES]
    if not masked:
        return window
    lane = lax.broadcasted_iota(jnp.int32, window.shape, 1) + low
    inside = (lane >= head * HD) & (lane < head * HD + HD)
    return jnp.where(inside, window, jnp.zeros_like(window))


def add_window(tiles_so_far, head, window):
    for place, tile in enumerate(head_tiles(head)):
        piece = window[:, place * LANES : (place + 1) * LANES]
        tiles_so_far[tile] = piece if tiles_so_far[tile] is None else tiles_so_far[tile] + piece


def kernel(
    sizes,
    hidden,
    cotangent,
    w_in,
    mod,
    gains,
    out_w,
    ones,
    grad_hidden,
    grad_w,
    hid_tok,
    cot_tok,
    gh_tok,
    weights,
    normed_s,
    rinv_s,
    q_s,
    k_s,
    v_s,
    rq_s,
    rk_s,
    qn_s,
    kn_s,
    att_s,
    ga_s,
    probs_s,
    x_send,
    x_recv,
    own_sem,
    w_send,
    w_recv,
    w_own,
):
    nseq, ndp, frames, chunks, tokens, width, gather_here = sizes
    mine = frames // nseq
    rows = frames * tokens
    block = chunks * tokens
    group = lax.axis_index("groups")
    seq = lax.axis_index("seq")
    dp = lax.axis_index("dp")
    core = lax.rem(seq, 2)
    sibling = seq + 1 - 2 * core
    seq_peers = [lax.rem(seq + i, nseq) for i in range(1, nseq)]

    barrier = pltpu.get_barrier_semaphore()
    count = nseq - 1
    for peer in seq_peers:
        pl.semaphore_signal(barrier, inc=1, device_id={"seq": peer}, device_id_type=MESH)
    if gather_here:
        for i in range(1, ndp):
            pl.semaphore_signal(
                barrier, inc=1, device_id={"dp": lax.rem(dp + i, ndp)}, device_id_type=MESH
            )
        pl.semaphore_signal(barrier, inc=1, device_id={"groups": 1 - group}, device_id_type=MESH)
        count += ndp
    pl.semaphore_wait(barrier, count)

    def frames_of(device):
        return pl.ds(device * mine, mine)

    def tokens_of(device, chunk):
        return pl.ds(pl.multiple_of(device * block + chunk * tokens, tokens), tokens)

    def inward(kind, chunk, i):
        source, target = ((hidden, hid_tok), (cotangent, cot_tok))[kind]
        return pltpu.make_async_remote_copy(
            src_ref=source.at[:, tokens_of(seq_peers[i], chunk), :],
            dst_ref=target.at[chunk, frames_of(seq)],
            send_sem=x_send.at[kind, chunk, i],
            recv_sem=x_recv.at[kind, chunk, i],
            device_id={"seq": seq_peers[i]},
            device_id_type=MESH,
        )

    def inward_own(kind, chunk):
        source, target = ((hidden, hid_tok), (cotangent, cot_tok))[kind]
        return pltpu.make_async_copy(
            source.at[:, tokens_of(seq, chunk), :],
            target.at[chunk, frames_of(seq)],
            own_sem.at[kind, chunk],
        )

    def outward(chunk, i):
        return pltpu.make_async_remote_copy(
            src_ref=gh_tok.at[chunk, frames_of(seq_peers[i])],
            dst_ref=grad_hidden.at[:, tokens_of(seq, chunk), :],
            send_sem=x_send.at[2, chunk, i],
            recv_sem=x_recv.at[2, chunk, i],
            device_id={"seq": seq_peers[i]},
            device_id_type=MESH,
        )

    def outward_own(chunk):
        return pltpu.make_async_copy(
            gh_tok.at[chunk, frames_of(seq)],
            grad_hidden.at[:, tokens_of(seq, chunk), :],
            own_sem.at[2, chunk],
        )

    shard = width // ndp
    half = shard // 2

    def piece(source, which):
        return weights.at[pl.ds(pl.multiple_of(source * shard + which * half, 16), half), :]

    def along_dp(i):
        return pltpu.make_async_remote_copy(
            src_ref=w_in.at[pl.ds(pl.multiple_of(group * half, 16), half), :],
            dst_ref=piece(dp, group),
            send_sem=w_send.at[0, i],
            recv_sem=w_recv.at[0, i],
            device_id={"dp": lax.rem(dp + i, ndp)},
            device_id_type=MESH,
        )

    def hand_on(step, i, which, target):
        source = lax.rem(dp + ndp - i, ndp)
        return pltpu.make_async_remote_copy(
            src_ref=piece(source, which),
            dst_ref=piece(source, which),
            send_sem=w_send.at[step, i],
            recv_sem=w_recv.at[step, i],
            device_id=target,
            device_id_type=MESH,
        )

    to_group = {"groups": 1 - group}
    to_core = {"seq": sibling}

    if gather_here:

        @pl.when(lax.rem(dp, 2) == core)
        def _():
            for i in range(1, ndp):
                along_dp(i).start()

        own_weights = pltpu.make_async_copy(
            w_in, weights.at[pl.ds(pl.multiple_of(dp * shard, 16), shard), :], w_own
        )
    else:
        own_weights = pltpu.make_async_copy(w_in, weights, w_own)
    for kind in range(2):
        for chunk in range(chunks):
            for i in range(nseq - 1):
                inward(kind, chunk, i).start()
    own_weights.start()
    for kind in range(2):
        for chunk in range(chunks):
            inward_own(kind, chunk).start()

    if gather_here:

        def relays(i):
            return lax.rem(lax.rem(dp + ndp - i, ndp), 2) == core

        for i in range(1, ndp):

            @pl.when(relays(i))
            def _():
                along_dp(i).wait_recv()
                hand_on(1, i, group, to_group).start()
                hand_on(2, i, group, to_core).start()

        for i in range(1, ndp):

            @pl.when(relays(i))
            def _():
                hand_on(1, i, 1 - group, to_group).wait_recv()
                hand_on(3, i, 1 - group, to_core).start()

        for i in range(1, ndp):

            @pl.when(jnp.logical_not(relays(i)))
            def _():
                hand_on(2, i, group, to_core).wait_recv()
                hand_on(3, i, 1 - group, to_core).wait_recv()

        for i in range(1, ndp):

            @pl.when(relays(i))
            def _():
                hand_on(1, i, group, to_group).wait_send()
                hand_on(2, i, group, to_core).wait_send()
                hand_on(3, i, 1 - group, to_core).wait_send()

        @pl.when(lax.rem(dp, 2) == core)
        def _():
            for i in range(1, ndp):
                along_dp(i).wait_send()

    own_weights.wait()

    scale = HD ** (-0.5)
    k_low = WIDE - (PAD - WIDE)
    v_low = 2 * WIDE

    def forward(chunk, carry):
        for i in range(nseq - 1):
            inward(0, chunk, i).wait()
        inward_own(0, chunk).wait()
        states = hid_tok[chunk].reshape(rows, width).astype(F32)
        centered = states - jnp.mean(states, -1, keepdims=True)
        rinv = lax.rsqrt(jnp.mean(centered * centered, -1, keepdims=True) + EPS)
        normed = centered * rinv
        normed_s[chunk] = normed
        rinv_s[chunk] = rinv
        modulated = (normed * (1.0 + mod[1:2, :]) + mod[0:1, :]).astype(BF16)
        q = dot_nn(modulated, weights[:, 0:PAD]).astype(BF16)
        k = pltpu.roll(dot_nn(modulated, weights[:, k_low : k_low + PAD]), WIDE, 1).astype(BF16)
        v = dot_nn(modulated, weights[:, v_low : v_low + WIDE]).astype(BF16)
        q_s[chunk] = q
        k_s[chunk] = k
        v = jnp.concatenate([v, jnp.zeros((rows, PAD - WIDE), BF16)], axis=1)
        v_s[chunk] = v
        q32 = q.astype(F32)
        k32 = k.astype(F32)
        rq = lax.rsqrt(head_sum(q32 * q32, ones[...]) * (1.0 / HD) + EPS)
        rk = lax.rsqrt(head_sum(k32 * k32, ones[...]) * (1.0 / HD) + EPS)
        rq_s[chunk] = rq
        rk_s[chunk] = rk
        qn = (q32 * rq * gains[0:1, :]).astype(BF16)
        kn = (k32 * rk * gains[1:2, :]).astype(BF16)
        qn_s[chunk] = qn
        kn_s[chunk] = kn
        down = lax.broadcasted_iota(jnp.int32, (rows, rows), 0)
        along = lax.broadcasted_iota(jnp.int32, (rows, rows), 1)
        same = ((down ^ along) & (tokens - 1)) == 0
        attended = [None] * (PAD // LANES)
        for head in range(HEADS):
            scores = dot_nt(head_window(kn, head, True), head_window(qn, head, False)) * scale
            scores = jnp.where(same, scores, -1e30)
            shifted = jnp.exp(scores - jnp.max(scores, 0, keepdims=True))
            probs = shifted * (1.0 / jnp.sum(shifted, 0, keepdims=True))
            probs_s[chunk, head] = probs
            add_window(attended, head, dot_tn(probs.astype(BF16), head_window(v, head, True)))
        att_s[chunk] = jnp.concatenate(attended, axis=1).astype(BF16)
        return carry

    lax.fori_loop(0, chunks, forward, 0)

    def middle(chunk, carry):
        for i in range(nseq - 1):
            inward(1, chunk, i).wait()
        inward_own(1, chunk).wait()
        gated = (mod[2:3, :] * cot_tok[chunk].reshape(rows, width).astype(F32)).astype(BF16)
        ga = dot_nt(gated, out_w[...]).astype(BF16)
        ga_s[chunk] = jnp.concatenate([ga, jnp.zeros((rows, PAD - WIDE), BF16)], axis=1)
        share = dot_tn(att_s[chunk][:, 0:WIDE], gated)

        @pl.when(chunk == 0)
        def _():
            grad_w[...] = share

        @pl.when(chunk > 0)
        def _():
            grad_w[...] += share

        return carry

    lax.fori_loop(0, chunks, middle, 0)

    def backward(chunk, carry):
        qn = qn_s[chunk]
        kn = kn_s[chunk]
        v = v_s[chunk]
        ga = ga_s[chunk]
        grad_qn = [None] * (PAD // LANES)
        grad_kn = [None] * (PAD // LANES)
        grad_v = [None] * (PAD // LANES)
        for head in range(HEADS):
            probs = probs_s[chunk, head]
            ga_head = head_window(ga, head, True)
            grad_probs = dot_nt(head_window(v, head, False), ga_head)
            total = jnp.sum(probs * grad_probs, 0, keepdims=True)
            grad_scores = (probs * (grad_probs - total) * scale).astype(BF16)
            add_window(grad_v, head, dot_nn(probs.astype(BF16), ga_head))
            add_window(grad_qn, head, dot_tn(grad_scores, head_window(kn, head, True)))
            add_window(grad_kn, head, dot_nn(grad_scores, head_window(qn, head, True)))

        def through_norm(raw, inverse, gain, grads):
            raw = raw.astype(F32)
            scaled = jnp.concatenate(grads, axis=1) * gain
            mean = head_sum(raw * scaled, ones[...]) * (1.0 / HD)
            return inverse * scaled - raw * inverse * inverse * inverse * mean

        grad_q = through_norm(q_s[chunk], rq_s[chunk], gains[0:1, :], grad_qn).astype(BF16)
        grad_k = pltpu.roll(
            through_norm(k_s[chunk], rk_s[chunk], gains[1:2, :], grad_kn), PAD - WIDE, 1
        ).astype(BF16)
        grad_v = jnp.concatenate(grad_v, axis=1)[:, 0:WIDE].astype(BF16)
        grad_mod = (
            dot_nt(grad_q, weights[:, 0:PAD])
            + dot_nt(grad_k, weights[:, k_low : k_low + PAD])
            + dot_nt(grad_v, weights[:, v_low : v_low + WIDE])
        ).astype(BF16)
        normed = normed_s[chunk]
        grad_normed = grad_mod.astype(F32) * (1.0 + mod[1:2, :])
        grad_ln = rinv_s[chunk] * (
            grad_normed
            - jnp.mean(grad_normed, -1, keepdims=True)
            - normed * jnp.mean(grad_normed * normed, -1, keepdims=True)
        )
        out = cot_tok[chunk].reshape(rows, width).astype(F32) + grad_ln
        gh_tok[chunk] = out.astype(BF16).reshape(frames, tokens, width)
        for i in range(nseq - 1):
            outward(chunk, i).start()
        outward_own(chunk).start()
        return carry

    lax.fori_loop(0, chunks, backward, 0)
    for chunk in range(chunks):
        for i in range(nseq - 1):
            outward(chunk, i).wait()
        outward_own(chunk).wait()


def shards(nseq, ndp, hidden_states, modulation, qkv_weight, qk_gain, out_weight, out_cotangent):
    mine, all_tokens, width = hidden_states.shape[1:]
    frames = mine * nseq
    block = all_tokens // nseq
    tokens = min(block, max(16, 256 // frames))
    chunks = block // tokens
    rows = frames * tokens
    gather_here = qkv_weight.shape[0] % 32 == 0
    if not gather_here:
        qkv_weight = lax.all_gather(qkv_weight, "dp", axis=0, tiled=True)
    gains = jnp.pad(jnp.tile(qk_gain, (1, HEADS)), ((0, 0), (0, PAD - WIDE)))
    lane = np.arange(PAD)
    inside = (lane < WIDE)[:, None] & (lane[:, None] // HD == lane[None, :] // HD)
    ones = jnp.asarray(inside.astype(np.float32), BF16)
    sizes = (nseq, ndp, frames, chunks, tokens, width, gather_here)
    anywhere = pl.BlockSpec(memory_space=pl.ANY)
    vmem = pl.BlockSpec(memory_space=pltpu.VMEM)

    def wide(dtype):
        return pltpu.VMEM((chunks, rows, PAD), dtype)

    by_token = pltpu.VMEM((chunks, frames, tokens, width), BF16)
    grad_hidden, share = pl.pallas_call(
        functools.partial(kernel, sizes),
        out_shape=(
            jax.ShapeDtypeStruct((mine, all_tokens, width), BF16),
            jax.ShapeDtypeStruct((WIDE, width), F32),
        ),
        in_specs=[anywhere, anywhere, anywhere, vmem, vmem, vmem, vmem],
        out_specs=(anywhere, vmem),
        scratch_shapes=[
            by_token,
            by_token,
            by_token,
            pltpu.VMEM((width, 3 * WIDE), BF16),
            pltpu.VMEM((chunks, rows, width), F32),
            pltpu.VMEM((chunks, rows, 1), F32),
            wide(BF16),
            wide(BF16),
            wide(BF16),
            wide(F32),
            wide(F32),
            wide(BF16),
            wide(BF16),
            wide(BF16),
            wide(BF16),
            pltpu.VMEM((chunks, HEADS, rows, rows), F32),
            pltpu.SemaphoreType.DMA((3, chunks, nseq - 1)),
            pltpu.SemaphoreType.DMA((3, chunks, nseq - 1)),
            pltpu.SemaphoreType.DMA((3, chunks)),
            pltpu.SemaphoreType.DMA((4, ndp)),
            pltpu.SemaphoreType.DMA((4, ndp)),
            pltpu.SemaphoreType.DMA,
        ],
        compiler_params=pltpu.CompilerParams(
            collective_id=0, has_side_effects=True, vmem_limit_bytes=56 * 2**20
        ),
        cost_estimate=pl.CostEstimate(
            flops=12_000_000_000, bytes_accessed=20_000_000, transcendentals=2_000_000
        ),
    )(hidden_states[0], out_cotangent[0], qkv_weight, modulation[0], gains, out_weight, ones)
    share = lax.psum_scatter(share, "seq", scatter_dimension=0, tiled=True)
    share = lax.psum_scatter(share, "dp", scatter_dimension=1, tiled=True)
    return (grad_hidden[None], share)


def solution(mesh):
    placed = (
        P(("groups", "dp"), "seq", None, None),
        P(("groups", "dp"), None, None),
        P("dp", None),
        P(),
        P(),
        P(("groups", "dp"), "seq", None, None),
    )
    return jax.shard_map(
        functools.partial(shards, mesh.shape["seq"], mesh.shape["dp"]),
        mesh=mesh,
        in_specs=placed,
        out_specs=(P(("groups", "dp"), "seq", None, None), P(("groups", "seq"), "dp")),
        check_vma=False,
    )
```

```python
import functools

import jax
import jax.numpy as jnp
import numpy as np
from jax import lax
from jax.experimental import pallas as pl
from jax.experimental.pallas import tpu as pltpu
from jax.sharding import PartitionSpec as P

HEADS = 8
HD = 72
WIDE = HEADS * HD
LANES = 128
PAD = -(-WIDE // LANES) * LANES
EPS = 1e-06
MESH = pl.DeviceIdType.MESH
F32 = jnp.float32
BF16 = jnp.bfloat16


def head_tiles(head):
    return range(head * HD // LANES, (head * HD + HD - 1) // LANES + 1)


def dot_nn(a, b):
    return lax.dot_general(a, b, (((1,), (0,)), ((), ())), preferred_element_type=F32)


def dot_nt(a, b):
    return lax.dot_general(a, b, (((1,), (1,)), ((), ())), preferred_element_type=F32)


def dot_tn(a, b):
    return lax.dot_general(a, b, (((0,), (0,)), ((), ())), preferred_element_type=F32)


def head_sum(values, ones):
    high = values.astype(BF16)
    low = (values - high.astype(F32)).astype(BF16)
    return dot_nn(high, ones) + dot_nn(low, ones)


def head_window(array, head, masked):
    tiles = head_tiles(head)
    low = tiles[0] * LANES
    window = array[:, low : low + len(tiles) * LANES]
    if not masked:
        return window
    lane = lax.broadcasted_iota(jnp.int32, window.shape, 1) + low
    inside = (lane >= head * HD) & (lane < head * HD + HD)
    return jnp.where(inside, window, jnp.zeros_like(window))


def add_window(tiles_so_far, head, window):
    for place, tile in enumerate(head_tiles(head)):
        piece = window[:, place * LANES : (place + 1) * LANES]
        tiles_so_far[tile] = piece if tiles_so_far[tile] is None else tiles_so_far[tile] + piece


def kernel(
    sizes,
    hidden,
    cotangent,
    w_in,
    mod,
    gain_in,
    out_w,
    ones,
    grad_hidden,
    grad_w,
    hid_tok,
    cot_tok,
    gh_tok,
    weights,
    normed_s,
    rinv_s,
    q_s,
    k_s,
    v_s,
    rq_s,
    rk_s,
    qn_s,
    kn_s,
    att_s,
    ga_s,
    probs_s,
    x_send,
    x_recv,
    own_sem,
    w_send,
    w_recv,
    w_own,
    share_s,
    pair_out,
    pair_in,
    far_out,
    far_in,
    col_out,
    col_in,
    g_send,
    g_recv,
):
    nseq, ndp, frames, chunks, tokens, width, gather_here, reduce_here = sizes
    mine = frames // nseq
    rows = frames * tokens
    block = chunks * tokens
    group = lax.axis_index("groups")
    seq = lax.axis_index("seq")
    dp = lax.axis_index("dp")
    core = lax.rem(seq, 2)
    sibling = seq + 1 - 2 * core
    seq_peers = [lax.rem(seq + i, nseq) for i in range(1, nseq)]

    barrier = pltpu.get_barrier_semaphore()
    count = nseq - 1
    for peer in seq_peers:
        pl.semaphore_signal(barrier, inc=1, device_id={"seq": peer}, device_id_type=MESH)
    if gather_here or reduce_here:
        for i in range(1, ndp):
            pl.semaphore_signal(
                barrier, inc=1, device_id={"dp": lax.rem(dp + i, ndp)}, device_id_type=MESH
            )
        count += ndp - 1
    if gather_here:
        pl.semaphore_signal(barrier, inc=1, device_id={"groups": 1 - group}, device_id_type=MESH)
        count += 1
    pl.semaphore_wait(barrier, count)

    def frames_of(device):
        return pl.ds(device * mine, mine)

    def tokens_of(device, chunk):
        return pl.ds(pl.multiple_of(device * block + chunk * tokens, tokens), tokens)

    def inward(kind, chunk, i):
        source, target = ((hidden, hid_tok), (cotangent, cot_tok))[kind]
        return pltpu.make_async_remote_copy(
            src_ref=source.at[:, tokens_of(seq_peers[i], chunk), :],
            dst_ref=target.at[chunk, frames_of(seq)],
            send_sem=x_send.at[kind, chunk, i],
            recv_sem=x_recv.at[kind, chunk, i],
            device_id={"seq": seq_peers[i]},
            device_id_type=MESH,
        )

    def inward_own(kind, chunk):
        source, target = ((hidden, hid_tok), (cotangent, cot_tok))[kind]
        return pltpu.make_async_copy(
            source.at[:, tokens_of(seq, chunk), :],
            target.at[chunk, frames_of(seq)],
            own_sem.at[kind, chunk],
        )

    def outward(chunk, i):
        return pltpu.make_async_remote_copy(
            src_ref=gh_tok.at[chunk, frames_of(seq_peers[i])],
            dst_ref=grad_hidden.at[:, tokens_of(seq, chunk), :],
            send_sem=x_send.at[2, chunk, i],
            recv_sem=x_recv.at[2, chunk, i],
            device_id={"seq": seq_peers[i]},
            device_id_type=MESH,
        )

    def outward_own(chunk):
        return pltpu.make_async_copy(
            gh_tok.at[chunk, frames_of(seq)],
            grad_hidden.at[:, tokens_of(seq, chunk), :],
            own_sem.at[2, chunk],
        )

    shard = width // ndp
    half = shard // 2

    def piece(source, which):
        return weights.at[pl.ds(pl.multiple_of(source * shard + which * half, 16), half), :]

    def along_dp(i):
        return pltpu.make_async_remote_copy(
            src_ref=w_in.at[pl.ds(pl.multiple_of(group * half, 16), half), :],
            dst_ref=piece(dp, group),
            send_sem=w_send.at[0, i],
            recv_sem=w_recv.at[0, i],
            device_id={"dp": lax.rem(dp + i, ndp)},
            device_id_type=MESH,
        )

    def hand_on(step, i, which, target):
        source = lax.rem(dp + ndp - i, ndp)
        return pltpu.make_async_remote_copy(
            src_ref=piece(source, which),
            dst_ref=piece(source, which),
            send_sem=w_send.at[step, i],
            recv_sem=w_recv.at[step, i],
            device_id=target,
            device_id_type=MESH,
        )

    to_group = {"groups": 1 - group}
    to_core = {"seq": sibling}

    if gather_here:

        @pl.when(lax.rem(dp, 2) == core)
        def _():
            for i in range(1, ndp):
                along_dp(i).start()

        own_weights = pltpu.make_async_copy(
            w_in, weights.at[pl.ds(pl.multiple_of(dp * shard, 16), shard), :], w_own
        )
    else:
        own_weights = pltpu.make_async_copy(w_in, weights, w_own)
    for kind in range(2):
        for chunk in range(chunks):
            for i in range(nseq - 1):
                inward(kind, chunk, i).start()
    own_weights.start()
    for kind in range(2):
        for chunk in range(chunks):
            inward_own(kind, chunk).start()

    if gather_here:

        def relays(i):
            return lax.rem(lax.rem(dp + ndp - i, ndp), 2) == core

        for i in range(1, ndp):

            @pl.when(relays(i))
            def _():
                along_dp(i).wait_recv()
                hand_on(1, i, group, to_group).start()
                hand_on(2, i, group, to_core).start()

        for i in range(1, ndp):

            @pl.when(relays(i))
            def _():
                hand_on(1, i, 1 - group, to_group).wait_recv()
                hand_on(3, i, 1 - group, to_core).start()

        for i in range(1, ndp):

            @pl.when(jnp.logical_not(relays(i)))
            def _():
                hand_on(2, i, group, to_core).wait_recv()
                hand_on(3, i, 1 - group, to_core).wait_recv()

        for i in range(1, ndp):

            @pl.when(relays(i))
            def _():
                hand_on(1, i, group, to_group).wait_send()
                hand_on(2, i, group, to_core).wait_send()
                hand_on(3, i, 1 - group, to_core).wait_send()

        @pl.when(lax.rem(dp, 2) == core)
        def _():
            for i in range(1, ndp):
                along_dp(i).wait_send()

    own_weights.wait()

    gains = jnp.concatenate([gain_in[...]] * HEADS + [jnp.zeros((2, PAD - WIDE), F32)], axis=1)
    scale = HD ** (-0.5)
    k_low = WIDE - (PAD - WIDE)
    v_low = 2 * WIDE

    def forward(chunk, carry):
        for i in range(nseq - 1):
            inward(0, chunk, i).wait()
        inward_own(0, chunk).wait()
        states = hid_tok[chunk].reshape(rows, width).astype(F32)
        centered = states - jnp.mean(states, -1, keepdims=True)
        rinv = lax.rsqrt(jnp.mean(centered * centered, -1, keepdims=True) + EPS)
        normed = centered * rinv
        normed_s[chunk] = normed
        rinv_s[chunk] = rinv
        modulated = (normed * (1.0 + mod[1:2, :]) + mod[0:1, :]).astype(BF16)
        q = dot_nn(modulated, weights[:, 0:PAD]).astype(BF16)
        k = pltpu.roll(dot_nn(modulated, weights[:, k_low : k_low + PAD]), WIDE, 1).astype(BF16)
        v = dot_nn(modulated, weights[:, v_low : v_low + WIDE]).astype(BF16)
        q_s[chunk] = q
        k_s[chunk] = k
        v = jnp.concatenate([v, jnp.zeros((rows, PAD - WIDE), BF16)], axis=1)
        v_s[chunk] = v
        q32 = q.astype(F32)
        k32 = k.astype(F32)
        rq = lax.rsqrt(head_sum(q32 * q32, ones[...]) * (1.0 / HD) + EPS)
        rk = lax.rsqrt(head_sum(k32 * k32, ones[...]) * (1.0 / HD) + EPS)
        rq_s[chunk] = rq
        rk_s[chunk] = rk
        qn = (q32 * rq * gains[0:1, :]).astype(BF16)
        kn = (k32 * rk * gains[1:2, :]).astype(BF16)
        qn_s[chunk] = qn
        kn_s[chunk] = kn
        down = lax.broadcasted_iota(jnp.int32, (rows, rows), 0)
        along = lax.broadcasted_iota(jnp.int32, (rows, rows), 1)
        same = ((down ^ along) & (tokens - 1)) == 0
        attended = [None] * (PAD // LANES)
        for head in range(HEADS):
            scores = dot_nt(head_window(kn, head, True), head_window(qn, head, False)) * scale
            scores = jnp.where(same, scores, -1e30)
            shifted = jnp.exp(scores - jnp.max(scores, 0, keepdims=True))
            probs = shifted * (1.0 / jnp.sum(shifted, 0, keepdims=True))
            probs_s[chunk, head] = probs
            add_window(attended, head, dot_tn(probs.astype(BF16), head_window(v, head, True)))
        att_s[chunk] = jnp.concatenate(attended, axis=1).astype(BF16)
        return carry

    lax.fori_loop(0, chunks, forward, 0)

    def middle(chunk, carry):
        for i in range(nseq - 1):
            inward(1, chunk, i).wait()
        inward_own(1, chunk).wait()
        gated = (mod[2:3, :] * cot_tok[chunk].reshape(rows, width).astype(F32)).astype(BF16)
        ga = dot_nt(gated, out_w[...]).astype(BF16)
        ga_s[chunk] = jnp.concatenate([ga, jnp.zeros((rows, PAD - WIDE), BF16)], axis=1)
        share = dot_tn(att_s[chunk][:, 0:WIDE], gated)
        target = share_s if reduce_here else grad_w
        share = share.reshape(target.shape)

        @pl.when(chunk == 0)
        def _():
            target[...] = share

        @pl.when(chunk > 0)
        def _():
            target[...] += share

        return carry

    lax.fori_loop(0, chunks, middle, 0)

    chips = nseq // 2
    chip = lax.div(seq, 2)
    columns = width // ndp

    def to_pair():
        return pltpu.make_async_remote_copy(
            src_ref=pair_out,
            dst_ref=pair_in,
            send_sem=g_send.at[0],
            recv_sem=g_recv.at[0],
            device_id=to_core,
            device_id_type=MESH,
        )

    def to_chip(i):
        return pltpu.make_async_remote_copy(
            src_ref=far_out.at[i - 1],
            dst_ref=far_in.at[i - 1],
            send_sem=g_send.at[i],
            recv_sem=g_recv.at[i],
            device_id={"seq": lax.rem(chip + i, chips) * 2 + core},
            device_id_type=MESH,
        )

    def to_columns(i):
        return pltpu.make_async_remote_copy(
            src_ref=col_out.at[lax.rem(dp + i, ndp)],
            dst_ref=col_in.at[i - 1],
            send_sem=g_send.at[chips + i - 1],
            recv_sem=g_recv.at[chips + i - 1],
            device_id={"dp": lax.rem(dp + i, ndp)},
            device_id_type=MESH,
        )

    def reduce_chips():
        to_pair().wait()
        for i in range(1, chips):
            there = lax.rem(chip + i, chips)
            far_out[i - 1] = (share_s[there * 2 + core] + pair_in[there].astype(F32)).astype(BF16)
            to_chip(i).start()

    def reduce_columns():
        total = share_s[seq] + pair_in[chip].astype(F32)
        for i in range(1, chips):
            to_chip(i).wait()
            total = total + far_in[i - 1].astype(F32)
        for d in range(ndp):
            part = total[:, d * columns : (d + 1) * columns]
            col_out[d] = part.astype(BF16)

            @pl.when(dp == d)
            def _():
                grad_w[...] = part

        for i in range(1, ndp):
            to_columns(i).start()

    if reduce_here:
        for c in range(chips):
            pair_out[c] = share_s[2 * c + 1 - core].astype(BF16)
        to_pair().start()

    def backward(chunk, carry):
        qn = qn_s[chunk]
        kn = kn_s[chunk]
        v = v_s[chunk]
        ga = ga_s[chunk]
        grad_qn = [None] * (PAD // LANES)
        grad_kn = [None] * (PAD // LANES)
        grad_v = [None] * (PAD // LANES)
        for head in range(HEADS):
            probs = probs_s[chunk, head]
            ga_head = head_window(ga, head, True)
            grad_probs = dot_nt(head_window(v, head, False), ga_head)
            total = jnp.sum(probs * grad_probs, 0, keepdims=True)
            grad_scores = (probs * (grad_probs - total) * scale).astype(BF16)
            add_window(grad_v, head, dot_nn(probs.astype(BF16), ga_head))
            add_window(grad_qn, head, dot_tn(grad_scores, head_window(kn, head, True)))
            add_window(grad_kn, head, dot_nn(grad_scores, head_window(qn, head, True)))

        def through_norm(raw, inverse, gain, grads):
            raw = raw.astype(F32)
            scaled = jnp.concatenate(grads, axis=1) * gain
            mean = head_sum(raw * scaled, ones[...]) * (1.0 / HD)
            return inverse * scaled - raw * inverse * inverse * inverse * mean

        grad_q = through_norm(q_s[chunk], rq_s[chunk], gains[0:1, :], grad_qn).astype(BF16)
        grad_k = pltpu.roll(
            through_norm(k_s[chunk], rk_s[chunk], gains[1:2, :], grad_kn), PAD - WIDE, 1
        ).astype(BF16)
        grad_v = jnp.concatenate(grad_v, axis=1)[:, 0:WIDE].astype(BF16)
        grad_mod = (
            dot_nt(grad_q, weights[:, 0:PAD])
            + dot_nt(grad_k, weights[:, k_low : k_low + PAD])
            + dot_nt(grad_v, weights[:, v_low : v_low + WIDE])
        ).astype(BF16)
        normed = normed_s[chunk]
        grad_normed = grad_mod.astype(F32) * (1.0 + mod[1:2, :])
        grad_ln = rinv_s[chunk] * (
            grad_normed
            - jnp.mean(grad_normed, -1, keepdims=True)
            - normed * jnp.mean(grad_normed * normed, -1, keepdims=True)
        )
        out = cot_tok[chunk].reshape(rows, width).astype(F32) + grad_ln
        gh_tok[chunk] = out.astype(BF16).reshape(frames, tokens, width)
        for i in range(nseq - 1):
            outward(chunk, i).start()
        outward_own(chunk).start()
        if reduce_here:

            @pl.when(chunk == 0)
            def _():
                reduce_chips()

        return carry

    lax.fori_loop(0, chunks, backward, 0)
    if reduce_here:
        reduce_columns()
        for i in range(1, ndp):
            to_columns(i).wait()
            grad_w[...] += col_in[i - 1].astype(F32)
    for chunk in range(chunks):
        for i in range(nseq - 1):
            outward(chunk, i).wait()
        outward_own(chunk).wait()


def shards(nseq, ndp, hidden_states, modulation, qkv_weight, qk_gain, out_weight, out_cotangent):
    mine, all_tokens, width = hidden_states.shape[1:]
    frames = mine * nseq
    block = all_tokens // nseq
    tokens = min(block, max(16, 256 // frames))
    chunks = block // tokens
    rows = frames * tokens
    gather_here = qkv_weight.shape[0] % 32 == 0
    if not gather_here:
        qkv_weight = lax.all_gather(qkv_weight, "dp", axis=0, tiled=True)
    lane = np.arange(PAD)
    inside = (lane < WIDE)[:, None] & (lane[:, None] // HD == lane[None, :] // HD)
    ones = jnp.asarray(inside.astype(np.float32), BF16)
    out_rows = WIDE // nseq
    columns = width // ndp
    reduce_here = out_rows % 16 == 0
    sizes = (nseq, ndp, frames, chunks, tokens, width, gather_here, reduce_here)
    if reduce_here:
        share_shape = (out_rows, columns)
        share_scratch = [
            pltpu.VMEM((nseq, out_rows, width), F32),
            pltpu.VMEM((nseq // 2, out_rows, width), BF16),
            pltpu.VMEM((nseq // 2, out_rows, width), BF16),
            pltpu.VMEM((nseq // 2 - 1, out_rows, width), BF16),
            pltpu.VMEM((nseq // 2 - 1, out_rows, width), BF16),
            pltpu.VMEM((ndp, out_rows, columns), BF16),
            pltpu.VMEM((ndp - 1, out_rows, columns), BF16),
        ]
    else:
        share_shape = (WIDE, width)
        share_scratch = [pltpu.VMEM((16, LANES), F32)] * 7
    anywhere = pl.BlockSpec(memory_space=pl.ANY)
    vmem = pl.BlockSpec(memory_space=pltpu.VMEM)

    def wide(dtype):
        return pltpu.VMEM((chunks, rows, PAD), dtype)

    by_token = pltpu.VMEM((chunks, frames, tokens, width), BF16)
    grad_hidden, share = pl.pallas_call(
        functools.partial(kernel, sizes),
        out_shape=(
            jax.ShapeDtypeStruct((mine, all_tokens, width), BF16),
            jax.ShapeDtypeStruct(share_shape, F32),
        ),
        in_specs=[anywhere, anywhere, anywhere, vmem, vmem, vmem, vmem],
        out_specs=(anywhere, vmem),
        scratch_shapes=[
            by_token,
            by_token,
            by_token,
            pltpu.VMEM((width, 3 * WIDE), BF16),
            pltpu.VMEM((chunks, rows, width), F32),
            pltpu.VMEM((chunks, rows, 1), F32),
            wide(BF16),
            wide(BF16),
            wide(BF16),
            wide(F32),
            wide(F32),
            wide(BF16),
            wide(BF16),
            wide(BF16),
            wide(BF16),
            pltpu.VMEM((chunks, HEADS, rows, rows), F32),
            pltpu.SemaphoreType.DMA((3, chunks, nseq - 1)),
            pltpu.SemaphoreType.DMA((3, chunks, nseq - 1)),
            pltpu.SemaphoreType.DMA((3, chunks)),
            pltpu.SemaphoreType.DMA((4, ndp)),
            pltpu.SemaphoreType.DMA((4, ndp)),
            pltpu.SemaphoreType.DMA,
            *share_scratch,
            pltpu.SemaphoreType.DMA((nseq // 2 + ndp,)),
            pltpu.SemaphoreType.DMA((nseq // 2 + ndp,)),
        ],
        compiler_params=pltpu.CompilerParams(
            collective_id=0, has_side_effects=True, vmem_limit_bytes=56 * 2**20
        ),
        cost_estimate=pl.CostEstimate(
            flops=12_000_000_000, bytes_accessed=20_000_000, transcendentals=2_000_000
        ),
    )(hidden_states[0], out_cotangent[0], qkv_weight, modulation[0], qk_gain, out_weight, ones)
    if not reduce_here:
        share = lax.psum_scatter(share, "seq", scatter_dimension=0, tiled=True)
        share = lax.psum_scatter(share, "dp", scatter_dimension=1, tiled=True)
    return (grad_hidden[None], share)


def solution(mesh):
    placed = (
        P(("groups", "dp"), "seq", None, None),
        P(("groups", "dp"), None, None),
        P("dp", None),
        P(),
        P(),
        P(("groups", "dp"), "seq", None, None),
    )
    return jax.shard_map(
        functools.partial(shards, mesh.shape["seq"], mesh.shape["dp"]),
        mesh=mesh,
        in_specs=placed,
        out_specs=(P(("groups", "dp"), "seq", None, None), P(("groups", "seq"), "dp")),
        check_vma=False,
    )
```

```python
import functools

import jax
import jax.numpy as jnp
import numpy as np
from jax import lax
from jax.experimental import pallas as pl
from jax.experimental.pallas import tpu as pltpu
from jax.sharding import PartitionSpec as P

HEADS = 8
HD = 72
WIDE = HEADS * HD
LANES = 128
PAD = -(-WIDE // LANES) * LANES
EPS = 1e-06
MESH = pl.DeviceIdType.MESH
F32 = jnp.float32
BF16 = jnp.bfloat16


def head_tiles(head):
    return range(head * HD // LANES, (head * HD + HD - 1) // LANES + 1)


def dot_nn(a, b):
    return lax.dot_general(a, b, (((1,), (0,)), ((), ())), preferred_element_type=F32)


def dot_nt(a, b):
    return lax.dot_general(a, b, (((1,), (1,)), ((), ())), preferred_element_type=F32)


def dot_tn(a, b):
    return lax.dot_general(a, b, (((0,), (0,)), ((), ())), preferred_element_type=F32)


def head_sum(values, ones):
    values = values.astype(BF16)
    parts = []
    for low in range(0, PAD, 256):
        high = min(low + 256, PAD)
        first = low // HD * HD // LANES * LANES
        last = min(-(-(-(-high // HD) * HD) // LANES) * LANES, PAD)
        parts.append(dot_nn(values[:, first:last], ones[first:last, low:high]))
    return jnp.concatenate(parts, axis=1)


def head_window(array, head, masked):
    tiles = head_tiles(head)
    low = tiles[0] * LANES
    window = array[:, low : low + len(tiles) * LANES]
    if not masked:
        return window
    lane = lax.broadcasted_iota(jnp.int32, window.shape, 1) + low
    inside = (lane >= head * HD) & (lane < head * HD + HD)
    return jnp.where(inside, window, jnp.zeros_like(window))


def add_window(tiles_so_far, head, window):
    for place, tile in enumerate(head_tiles(head)):
        piece = window[:, place * LANES : (place + 1) * LANES]
        tiles_so_far[tile] = piece if tiles_so_far[tile] is None else tiles_so_far[tile] + piece


def kernel(
    sizes,
    hidden,
    cotangent,
    w_in,
    mod,
    gain_in,
    out_w,
    ones,
    grad_hidden,
    grad_w,
    hid_tok,
    cot_tok,
    gh_tok,
    weights,
    normed_s,
    modulated_s,
    rinv_s,
    q_s,
    k_s,
    v_s,
    rq_s,
    rk_s,
    qn_s,
    kn_s,
    att_s,
    ga_s,
    probs_s,
    x_send,
    x_recv,
    own_sem,
    w_send,
    w_recv,
    w_own,
    share_s,
    pair_out,
    pair_in,
    far_out,
    far_in,
    col_out,
    col_in,
    g_send,
    g_recv,
):
    nseq, ndp, frames, chunks, tokens, width, gather_here, reduce_here = sizes
    mine = frames // nseq
    rows = frames * tokens
    block = chunks * tokens
    group = lax.axis_index("groups")
    seq = lax.axis_index("seq")
    dp = lax.axis_index("dp")
    core = lax.rem(seq, 2)
    sibling = seq + 1 - 2 * core
    seq_peers = [lax.rem(seq + i, nseq) for i in range(1, nseq)]

    barrier = pltpu.get_barrier_semaphore()
    count = nseq - 1
    for peer in seq_peers:
        pl.semaphore_signal(barrier, inc=1, device_id={"seq": peer}, device_id_type=MESH)
    if gather_here or reduce_here:
        for i in range(1, ndp):
            pl.semaphore_signal(
                barrier, inc=1, device_id={"dp": lax.rem(dp + i, ndp)}, device_id_type=MESH
            )
        count += ndp - 1
    if gather_here:
        pl.semaphore_signal(barrier, inc=1, device_id={"groups": 1 - group}, device_id_type=MESH)
        count += 1
    pl.semaphore_wait(barrier, count)

    def frames_of(device):
        return pl.ds(device * mine, mine)

    def tokens_of(device, chunk):
        return pl.ds(pl.multiple_of(device * block + chunk * tokens, tokens), tokens)

    def inward(kind, chunk, i):
        source, target = ((hidden, hid_tok), (cotangent, cot_tok))[kind]
        return pltpu.make_async_remote_copy(
            src_ref=source.at[:, tokens_of(seq_peers[i], chunk), :],
            dst_ref=target.at[chunk, frames_of(seq)],
            send_sem=x_send.at[kind, chunk, i],
            recv_sem=x_recv.at[kind, chunk, i],
            device_id={"seq": seq_peers[i]},
            device_id_type=MESH,
        )

    def inward_own(kind, chunk):
        source, target = ((hidden, hid_tok), (cotangent, cot_tok))[kind]
        return pltpu.make_async_copy(
            source.at[:, tokens_of(seq, chunk), :],
            target.at[chunk, frames_of(seq)],
            own_sem.at[kind, chunk],
        )

    def outward(chunk, i):
        return pltpu.make_async_remote_copy(
            src_ref=gh_tok.at[chunk, frames_of(seq_peers[i])],
            dst_ref=grad_hidden.at[:, tokens_of(seq, chunk), :],
            send_sem=x_send.at[2, chunk, i],
            recv_sem=x_recv.at[2, chunk, i],
            device_id={"seq": seq_peers[i]},
            device_id_type=MESH,
        )

    def outward_own(chunk):
        return pltpu.make_async_copy(
            gh_tok.at[chunk, frames_of(seq)],
            grad_hidden.at[:, tokens_of(seq, chunk), :],
            own_sem.at[2, chunk],
        )

    shard = width // ndp
    half = shard // 2

    def piece(source, which):
        return weights.at[pl.ds(pl.multiple_of(source * shard + which * half, 16), half), :]

    def along_dp(i):
        return pltpu.make_async_remote_copy(
            src_ref=w_in.at[pl.ds(pl.multiple_of(group * half, 16), half), :],
            dst_ref=piece(dp, group),
            send_sem=w_send.at[0, i],
            recv_sem=w_recv.at[0, i],
            device_id={"dp": lax.rem(dp + i, ndp)},
            device_id_type=MESH,
        )

    def hand_on(step, i, which, target):
        source = lax.rem(dp + ndp - i, ndp)
        return pltpu.make_async_remote_copy(
            src_ref=piece(source, which),
            dst_ref=piece(source, which),
            send_sem=w_send.at[step, i],
            recv_sem=w_recv.at[step, i],
            device_id=target,
            device_id_type=MESH,
        )

    to_group = {"groups": 1 - group}
    to_core = {"seq": sibling}

    if gather_here:

        @pl.when(lax.rem(dp, 2) == core)
        def _():
            for i in range(1, ndp):
                along_dp(i).start()

        own_weights = pltpu.make_async_copy(
            w_in, weights.at[pl.ds(pl.multiple_of(dp * shard, 16), shard), :], w_own
        )
    else:
        own_weights = pltpu.make_async_copy(w_in, weights, w_own)
    for chunk in range(chunks):
        for i in range(nseq - 1):
            inward(0, chunk, i).start()
    own_weights.start()
    for kind in range(2):
        for chunk in range(chunks):
            inward_own(kind, chunk).start()

    def norm(chunk, carry):
        for i in range(nseq - 1):
            inward(0, chunk, i).wait()
        inward_own(0, chunk).wait()
        states = hid_tok[chunk].reshape(rows, width).astype(F32)
        centered = states - jnp.mean(states, -1, keepdims=True)
        rinv = lax.rsqrt(jnp.mean(centered * centered, -1, keepdims=True) + EPS)
        normed = centered * rinv
        normed_s[chunk] = normed
        rinv_s[chunk] = rinv
        modulated_s[chunk] = (normed * (1.0 + mod[1]) + mod[0]).astype(BF16)
        return carry

    def second_array():
        for chunk in range(chunks):
            for i in range(nseq - 1):
                inward(1, chunk, i).start()

    if gather_here:
        order = [jnp.where(dp == 0, ndp - i, i) for i in range(1, ndp)]

        def relays(i):
            return lax.rem(lax.rem(dp + ndp - i, ndp), 2) == core

        def from_dp(i):
            @pl.when(relays(i))
            def _():
                along_dp(i).wait_recv()
                hand_on(1, i, group, to_group).start()
                hand_on(2, i, group, to_core).start()

        def from_group(i):
            @pl.when(relays(i))
            def _():
                hand_on(1, i, 1 - group, to_group).wait_recv()
                hand_on(3, i, 1 - group, to_core).start()

        from_dp(order[0])
        lax.fori_loop(0, chunks, norm, 0)
        second_array()
        for i in order[1:]:
            from_dp(i)
        for i in order:
            from_group(i)
        for i in order:

            @pl.when(jnp.logical_not(relays(i)))
            def _():
                hand_on(2, i, group, to_core).wait_recv()
                hand_on(3, i, 1 - group, to_core).wait_recv()

    else:
        lax.fori_loop(0, chunks, norm, 0)
        second_array()
    own_weights.wait()

    gains = jnp.concatenate([gain_in[...]] * HEADS + [jnp.zeros((2, PAD - WIDE), F32)], axis=1)
    scale = HD ** (-0.5)
    k_low = WIDE - (PAD - WIDE)
    v_low = 2 * WIDE

    def forward(chunk, carry):
        modulated = modulated_s[chunk]
        q = dot_nn(modulated, weights[:, 0:PAD]).astype(BF16)
        k = pltpu.roll(dot_nn(modulated, weights[:, k_low : k_low + PAD]), WIDE, 1).astype(BF16)
        v = dot_nn(modulated, weights[:, v_low : v_low + WIDE]).astype(BF16)
        q_s[chunk] = q
        k_s[chunk] = k
        v = jnp.concatenate([v, jnp.zeros((rows, PAD - WIDE), BF16)], axis=1)
        v_s[chunk] = v
        q32 = q.astype(F32)
        k32 = k.astype(F32)
        rq = lax.rsqrt(head_sum(q32 * q32, ones) * (1.0 / HD) + EPS)
        rk = lax.rsqrt(head_sum(k32 * k32, ones) * (1.0 / HD) + EPS)
        rq_s[chunk] = rq
        rk_s[chunk] = rk
        qn = (q32 * rq * gains[0:1, :]).astype(BF16)
        kn = (k32 * rk * gains[1:2, :]).astype(BF16)
        qn_s[chunk] = qn
        kn_s[chunk] = kn
        down = lax.broadcasted_iota(jnp.int32, (rows, rows), 0)
        along = lax.broadcasted_iota(jnp.int32, (rows, rows), 1)
        same = ((down ^ along) & (tokens - 1)) == 0
        attended = [None] * (PAD // LANES)
        for head in range(HEADS):
            scores = dot_nt(head_window(kn, head, True), head_window(qn, head, False)) * scale
            scores = jnp.where(same, scores, -1e30)
            shifted = jnp.exp(scores - jnp.max(scores, 0, keepdims=True))
            probs = shifted * (1.0 / jnp.sum(shifted, 0, keepdims=True))
            probs_s[chunk, head] = probs
            add_window(attended, head, dot_tn(probs.astype(BF16), head_window(v, head, True)))
        att_s[chunk] = jnp.concatenate(attended, axis=1).astype(BF16)
        return carry

    lax.fori_loop(0, chunks, forward, 0)

    def middle(chunk, carry):
        for i in range(nseq - 1):
            inward(1, chunk, i).wait()
        inward_own(1, chunk).wait()
        gated = (mod[2] * cot_tok[chunk].reshape(rows, width).astype(F32)).astype(BF16)
        ga = dot_nt(gated, out_w[...]).astype(BF16)
        ga_s[chunk] = jnp.concatenate([ga, jnp.zeros((rows, PAD - WIDE), BF16)], axis=1)
        share = dot_tn(att_s[chunk][:, 0:WIDE], gated)
        target = share_s if reduce_here else grad_w
        share = share.reshape(target.shape)

        @pl.when(chunk == 0)
        def _():
            target[...] = share

        @pl.when(chunk > 0)
        def _():
            target[...] += share

        return carry

    lax.fori_loop(0, chunks, middle, 0)

    chips = nseq // 2
    chip = lax.div(seq, 2)
    columns = width // ndp

    def to_pair():
        return pltpu.make_async_remote_copy(
            src_ref=pair_out,
            dst_ref=pair_in,
            send_sem=g_send.at[0],
            recv_sem=g_recv.at[0],
            device_id=to_core,
            device_id_type=MESH,
        )

    def to_chip(i):
        return pltpu.make_async_remote_copy(
            src_ref=far_out.at[i - 1],
            dst_ref=far_in.at[i - 1],
            send_sem=g_send.at[i],
            recv_sem=g_recv.at[i],
            device_id={"seq": lax.rem(chip + i, chips) * 2 + core},
            device_id_type=MESH,
        )

    def to_columns(i):
        return pltpu.make_async_remote_copy(
            src_ref=col_out.at[lax.rem(dp + i, ndp)],
            dst_ref=col_in.at[i - 1],
            send_sem=g_send.at[chips + i - 1],
            recv_sem=g_recv.at[chips + i - 1],
            device_id={"dp": lax.rem(dp + i, ndp)},
            device_id_type=MESH,
        )

    def reduce_chips():
        to_pair().wait()
        for i in range(1, chips):
            there = lax.rem(chip + i, chips)
            far_out[i - 1] = (share_s[there * 2 + core] + pair_in[there].astype(F32)).astype(BF16)
            to_chip(i).start()

    def reduce_columns():
        total = share_s[seq] + pair_in[chip].astype(F32)
        for i in range(1, chips):
            to_chip(i).wait()
            total = total + far_in[i - 1].astype(F32)
        for d in range(ndp):
            part = total[:, d * columns : (d + 1) * columns]
            col_out[d] = part.astype(BF16)

            @pl.when(dp == d)
            def _():
                grad_w[...] = part

        for i in range(1, ndp):
            to_columns(i).start()

    if reduce_here:
        for c in range(chips):
            pair_out[c] = share_s[2 * c + 1 - core].astype(BF16)
        to_pair().start()

    def backward(chunk, carry):
        qn = qn_s[chunk]
        kn = kn_s[chunk]
        v = v_s[chunk]
        ga = ga_s[chunk]
        grad_qn = [None] * (PAD // LANES)
        grad_kn = [None] * (PAD // LANES)
        grad_v = [None] * (PAD // LANES)
        for head in range(HEADS):
            probs = probs_s[chunk, head]
            ga_head = head_window(ga, head, True)
            grad_probs = dot_nt(head_window(v, head, False), ga_head)
            total = jnp.sum(probs * grad_probs, 0, keepdims=True)
            grad_scores = (probs * (grad_probs - total) * scale).astype(BF16)
            add_window(grad_v, head, dot_nn(probs.astype(BF16), ga_head))
            add_window(grad_qn, head, dot_tn(grad_scores, head_window(kn, head, True)))
            add_window(grad_kn, head, dot_nn(grad_scores, head_window(qn, head, True)))

        def through_norm(raw, inverse, gain, grads):
            raw = raw.astype(F32)
            scaled = jnp.concatenate(grads, axis=1) * gain
            mean = head_sum(raw * scaled, ones) * (1.0 / HD)
            return inverse * scaled - raw * inverse * inverse * inverse * mean

        grad_q = through_norm(q_s[chunk], rq_s[chunk], gains[0:1, :], grad_qn).astype(BF16)
        grad_k = pltpu.roll(
            through_norm(k_s[chunk], rk_s[chunk], gains[1:2, :], grad_kn), PAD - WIDE, 1
        ).astype(BF16)
        grad_v = jnp.concatenate(grad_v, axis=1)[:, 0:WIDE].astype(BF16)
        grad_mod = (
            dot_nt(grad_q, weights[:, 0:PAD])
            + dot_nt(grad_k, weights[:, k_low : k_low + PAD])
            + dot_nt(grad_v, weights[:, v_low : v_low + WIDE])
        ).astype(BF16)
        normed = normed_s[chunk]
        grad_normed = grad_mod.astype(F32) * (1.0 + mod[1])
        grad_ln = rinv_s[chunk] * (
            grad_normed
            - jnp.mean(grad_normed, -1, keepdims=True)
            - normed * jnp.mean(grad_normed * normed, -1, keepdims=True)
        )
        out = cot_tok[chunk].reshape(rows, width).astype(F32) + grad_ln
        gh_tok[chunk] = out.astype(BF16).reshape(frames, tokens, width)
        for i in range(nseq - 1):
            outward(chunk, i).start()
        outward_own(chunk).start()
        if reduce_here:

            @pl.when(chunk == 0)
            def _():
                reduce_chips()

        return carry

    lax.fori_loop(0, chunks, backward, 0)
    if reduce_here:
        reduce_columns()
        for i in range(1, ndp):
            to_columns(i).wait()
            grad_w[...] += col_in[i - 1].astype(F32)
    if gather_here:
        for i in order:

            @pl.when(relays(i))
            def _():
                hand_on(1, i, group, to_group).wait_send()
                hand_on(2, i, group, to_core).wait_send()
                hand_on(3, i, 1 - group, to_core).wait_send()

        @pl.when(lax.rem(dp, 2) == core)
        def _():
            for i in range(1, ndp):
                along_dp(i).wait_send()

    for chunk in range(chunks):
        for i in range(nseq - 1):
            outward(chunk, i).wait()
        outward_own(chunk).wait()


def shards(nseq, ndp, hidden_states, modulation, qkv_weight, qk_gain, out_weight, out_cotangent):
    mine, all_tokens, width = hidden_states.shape[1:]
    frames = mine * nseq
    block = all_tokens // nseq
    tokens = min(block, max(16, 256 // frames))
    chunks = block // tokens
    rows = frames * tokens
    gather_here = qkv_weight.shape[0] % 32 == 0
    if not gather_here:
        qkv_weight = lax.all_gather(qkv_weight, "dp", axis=0, tiled=True)
    lane = np.arange(PAD)
    inside = (lane < WIDE)[:, None] & (lane[:, None] // HD == lane[None, :] // HD)
    ones = jnp.asarray(inside.astype(np.float32), BF16)
    out_rows = WIDE // nseq
    columns = width // ndp
    reduce_here = out_rows % 16 == 0
    sizes = (nseq, ndp, frames, chunks, tokens, width, gather_here, reduce_here)
    if reduce_here:
        share_shape = (out_rows, columns)
        share_scratch = [
            pltpu.VMEM((nseq, out_rows, width), F32),
            pltpu.VMEM((nseq // 2, out_rows, width), BF16),
            pltpu.VMEM((nseq // 2, out_rows, width), BF16),
            pltpu.VMEM((nseq // 2 - 1, out_rows, width), BF16),
            pltpu.VMEM((nseq // 2 - 1, out_rows, width), BF16),
            pltpu.VMEM((ndp, out_rows, columns), BF16),
            pltpu.VMEM((ndp - 1, out_rows, columns), BF16),
        ]
    else:
        share_shape = (WIDE, width)
        share_scratch = [pltpu.VMEM((16, LANES), F32)] * 7
    anywhere = pl.BlockSpec(memory_space=pl.ANY)
    vmem = pl.BlockSpec(memory_space=pltpu.VMEM)

    def wide(dtype):
        return pltpu.VMEM((chunks, rows, PAD), dtype)

    by_token = pltpu.VMEM((chunks, frames, tokens, width), BF16)
    grad_hidden, share = pl.pallas_call(
        functools.partial(kernel, sizes),
        out_shape=(
            jax.ShapeDtypeStruct((mine, all_tokens, width), BF16),
            jax.ShapeDtypeStruct(share_shape, F32),
        ),
        in_specs=[anywhere, anywhere, anywhere, vmem, vmem, vmem, vmem],
        out_specs=(anywhere, vmem),
        scratch_shapes=[
            by_token,
            by_token,
            by_token,
            pltpu.VMEM((width, 3 * WIDE), BF16),
            pltpu.VMEM((chunks, rows, width), F32),
            pltpu.VMEM((chunks, rows, width), BF16),
            pltpu.VMEM((chunks, rows, 1), F32),
            wide(BF16),
            wide(BF16),
            wide(BF16),
            wide(F32),
            wide(F32),
            wide(BF16),
            wide(BF16),
            wide(BF16),
            wide(BF16),
            pltpu.VMEM((chunks, HEADS, rows, rows), F32),
            pltpu.SemaphoreType.DMA((3, chunks, nseq - 1)),
            pltpu.SemaphoreType.DMA((3, chunks, nseq - 1)),
            pltpu.SemaphoreType.DMA((3, chunks)),
            pltpu.SemaphoreType.DMA((4, ndp)),
            pltpu.SemaphoreType.DMA((4, ndp)),
            pltpu.SemaphoreType.DMA,
            *share_scratch,
            pltpu.SemaphoreType.DMA((nseq // 2 + ndp,)),
            pltpu.SemaphoreType.DMA((nseq // 2 + ndp,)),
        ],
        compiler_params=pltpu.CompilerParams(
            collective_id=0, has_side_effects=True, vmem_limit_bytes=56 * 2**20
        ),
        cost_estimate=pl.CostEstimate(
            flops=12_000_000_000, bytes_accessed=20_000_000, transcendentals=2_000_000
        ),
    )(hidden_states[0], out_cotangent[0], qkv_weight, modulation.transpose(1, 0, 2), qk_gain, out_weight, ones)
    if not reduce_here:
        share = lax.psum_scatter(share, "seq", scatter_dimension=0, tiled=True)
        share = lax.psum_scatter(share, "dp", scatter_dimension=1, tiled=True)
    return (grad_hidden[None], share)


def solution(mesh):
    placed = (
        P(("groups", "dp"), "seq", None, None),
        P(("groups", "dp"), None, None),
        P("dp", None),
        P(),
        P(),
        P(("groups", "dp"), "seq", None, None),
    )
    return jax.shard_map(
        functools.partial(shards, mesh.shape["seq"], mesh.shape["dp"]),
        mesh=mesh,
        in_specs=placed,
        out_specs=(P(("groups", "dp"), "seq", None, None), P(("groups", "seq"), "dp")),
        check_vma=False,
    )
```

```python
import functools

import jax
import jax.numpy as jnp
import numpy as np
from jax import lax
from jax.experimental import pallas as pl
from jax.experimental.pallas import tpu as pltpu
from jax.sharding import PartitionSpec as P

HEADS = 8
HD = 72
WIDE = HEADS * HD
LANES = 128
PAD = -(-WIDE // LANES) * LANES
EPS = 1e-06
MESH = pl.DeviceIdType.MESH
F32 = jnp.float32
BF16 = jnp.bfloat16


def head_tiles(head):
    return range(head * HD // LANES, (head * HD + HD - 1) // LANES + 1)


def dot_nn(a, b):
    return lax.dot_general(a, b, (((1,), (0,)), ((), ())), preferred_element_type=F32)


def dot_nt(a, b):
    return lax.dot_general(a, b, (((1,), (1,)), ((), ())), preferred_element_type=F32)


def dot_tn(a, b):
    return lax.dot_general(a, b, (((0,), (0,)), ((), ())), preferred_element_type=F32)


def head_sum(values, ones):
    values = values.astype(BF16)
    parts = []
    for low in range(0, PAD, 256):
        high = min(low + 256, PAD)
        first = low // HD * HD // LANES * LANES
        last = min(-(-(-(-high // HD) * HD) // LANES) * LANES, PAD)
        parts.append(dot_nn(values[:, first:last], ones[first:last, low:high]))
    return jnp.concatenate(parts, axis=1)


def head_window(array, head, masked):
    tiles = head_tiles(head)
    low = tiles[0] * LANES
    window = array[:, low : low + len(tiles) * LANES]
    if not masked:
        return window
    lane = lax.broadcasted_iota(jnp.int32, window.shape, 1) + low
    inside = (lane >= head * HD) & (lane < head * HD + HD)
    return jnp.where(inside, window, jnp.zeros_like(window))


def add_window(tiles_so_far, head, window):
    for place, tile in enumerate(head_tiles(head)):
        piece = window[:, place * LANES : (place + 1) * LANES]
        tiles_so_far[tile] = piece if tiles_so_far[tile] is None else tiles_so_far[tile] + piece


def kernel(
    sizes,
    hidden,
    cotangent,
    w_in,
    mod,
    gain_in,
    out_w,
    ones,
    grad_hidden,
    grad_w,
    hid_tok,
    cot_tok,
    gh_tok,
    weights,
    normed_s,
    modulated_s,
    rinv_s,
    q_s,
    k_s,
    v_s,
    rq_s,
    rk_s,
    qn_s,
    kn_s,
    att_s,
    ga_s,
    probs_s,
    x_send,
    x_recv,
    own_sem,
    w_send,
    w_recv,
    w_own,
    share_s,
    pair_out,
    pair_in,
    far_out,
    far_in,
    col_out,
    col_in,
    g_send,
    g_recv,
):
    nseq, ndp, frames, chunks, tokens, width, gather_here, reduce_here = sizes
    mine = frames // nseq
    rows = frames * tokens
    block = chunks * tokens
    group = lax.axis_index("groups")
    seq = lax.axis_index("seq")
    dp = lax.axis_index("dp")
    core = lax.rem(seq, 2)
    sibling = seq + 1 - 2 * core
    seq_peers = [lax.rem(seq + i, nseq) for i in range(1, nseq)]

    barrier = pltpu.get_barrier_semaphore()
    count = nseq - 1
    for peer in seq_peers:
        pl.semaphore_signal(barrier, inc=1, device_id={"seq": peer}, device_id_type=MESH)
    if gather_here or reduce_here:
        for i in range(1, ndp):
            pl.semaphore_signal(
                barrier, inc=1, device_id={"dp": lax.rem(dp + i, ndp)}, device_id_type=MESH
            )
        count += ndp - 1
    if gather_here:
        pl.semaphore_signal(barrier, inc=1, device_id={"groups": 1 - group}, device_id_type=MESH)
        count += 1
    pl.semaphore_wait(barrier, count)

    def frames_of(device):
        return pl.ds(device * mine, mine)

    def tokens_of(device, chunk):
        return pl.ds(pl.multiple_of(device * block + chunk * tokens, tokens), tokens)

    def inward(kind, chunk, i):
        source, target = ((hidden, hid_tok), (cotangent, cot_tok))[kind]
        return pltpu.make_async_remote_copy(
            src_ref=source.at[:, tokens_of(seq_peers[i], chunk), :],
            dst_ref=target.at[chunk, frames_of(seq)],
            send_sem=x_send.at[kind, chunk, i],
            recv_sem=x_recv.at[kind, chunk, i],
            device_id={"seq": seq_peers[i]},
            device_id_type=MESH,
        )

    def inward_own(kind, chunk):
        source, target = ((hidden, hid_tok), (cotangent, cot_tok))[kind]
        return pltpu.make_async_copy(
            source.at[:, tokens_of(seq, chunk), :],
            target.at[chunk, frames_of(seq)],
            own_sem.at[kind, chunk],
        )

    def outward(chunk, i):
        return pltpu.make_async_remote_copy(
            src_ref=gh_tok.at[chunk, frames_of(seq_peers[i])],
            dst_ref=grad_hidden.at[:, tokens_of(seq, chunk), :],
            send_sem=x_send.at[2, chunk, i],
            recv_sem=x_recv.at[2, chunk, i],
            device_id={"seq": seq_peers[i]},
            device_id_type=MESH,
        )

    def outward_own(chunk):
        return pltpu.make_async_copy(
            gh_tok.at[chunk, frames_of(seq)],
            grad_hidden.at[:, tokens_of(seq, chunk), :],
            own_sem.at[2, chunk],
        )

    shard = width // ndp
    half = shard // 2

    def piece(source, which):
        return weights.at[pl.ds(pl.multiple_of(source * shard + which * half, 16), half), :]

    def along_dp(i):
        return pltpu.make_async_remote_copy(
            src_ref=w_in.at[pl.ds(pl.multiple_of(group * half, 16), half), :],
            dst_ref=piece(dp, group),
            send_sem=w_send.at[0, i],
            recv_sem=w_recv.at[0, i],
            device_id={"dp": lax.rem(dp + i, ndp)},
            device_id_type=MESH,
        )

    def hand_on(step, i, which, target):
        source = lax.rem(dp + ndp - i, ndp)
        return pltpu.make_async_remote_copy(
            src_ref=piece(source, which),
            dst_ref=piece(source, which),
            send_sem=w_send.at[step, i],
            recv_sem=w_recv.at[step, i],
            device_id=target,
            device_id_type=MESH,
        )

    to_group = {"groups": 1 - group}
    to_core = {"seq": sibling}

    if gather_here:

        @pl.when(lax.rem(dp, 2) == core)
        def _():
            for i in range(1, ndp):
                along_dp(i).start()

        own_weights = pltpu.make_async_copy(
            w_in, weights.at[pl.ds(pl.multiple_of(dp * shard, 16), shard), :], w_own
        )
    else:
        own_weights = pltpu.make_async_copy(w_in, weights, w_own)
    for chunk in range(chunks):
        for i in range(nseq - 1):
            inward(0, chunk, i).start()
    own_weights.start()
    for kind in range(2):
        for chunk in range(chunks):
            inward_own(kind, chunk).start()

    def norm(chunk, carry):
        for i in range(nseq - 1):
            inward(0, chunk, i).wait()
        inward_own(0, chunk).wait()
        states = hid_tok[chunk].reshape(rows, width).astype(F32)
        centered = states - jnp.mean(states, -1, keepdims=True)
        rinv = lax.rsqrt(jnp.mean(centered * centered, -1, keepdims=True) + EPS)
        normed = centered * rinv
        normed_s[chunk] = normed
        rinv_s[chunk] = rinv
        modulated_s[chunk] = (normed * (1.0 + mod[1]) + mod[0]).astype(BF16)
        return carry

    def second_array():
        for chunk in range(chunks):
            for i in range(nseq - 1):
                inward(1, chunk, i).start()

    if gather_here:
        order = [jnp.where(dp == 0, ndp - i, i) for i in range(1, ndp)]

        def relays(i):
            return lax.rem(lax.rem(dp + ndp - i, ndp), 2) == core

        def from_dp(i):
            @pl.when(relays(i))
            def _():
                along_dp(i).wait_recv()
                hand_on(1, i, group, to_group).start()
                hand_on(2, i, group, to_core).start()

        def from_group(i):
            @pl.when(relays(i))
            def _():
                hand_on(1, i, 1 - group, to_group).wait_recv()
                hand_on(3, i, 1 - group, to_core).start()

        from_dp(order[0])
        lax.fori_loop(0, chunks, norm, 0)
        second_array()
        from_group(order[0])
        for i in order[1:]:
            from_dp(i)
        for i in order[1:]:
            from_group(i)
        for i in order:

            @pl.when(jnp.logical_not(relays(i)))
            def _():
                hand_on(2, i, group, to_core).wait_recv()
                hand_on(3, i, 1 - group, to_core).wait_recv()

    else:
        lax.fori_loop(0, chunks, norm, 0)
        second_array()
    own_weights.wait()

    gains = jnp.concatenate([gain_in[...]] * HEADS + [jnp.zeros((2, PAD - WIDE), F32)], axis=1)
    scale = HD ** (-0.5)
    k_low = WIDE - (PAD - WIDE)
    v_low = 2 * WIDE

    def forward(chunk, carry):
        modulated = modulated_s[chunk]
        q = dot_nn(modulated, weights[:, 0:PAD]).astype(BF16)
        k = pltpu.roll(dot_nn(modulated, weights[:, k_low : k_low + PAD]), WIDE, 1).astype(BF16)
        v = dot_nn(modulated, weights[:, v_low : v_low + WIDE]).astype(BF16)
        q_s[chunk] = q
        k_s[chunk] = k
        v = jnp.concatenate([v, jnp.zeros((rows, PAD - WIDE), BF16)], axis=1)
        v_s[chunk] = v
        q32 = q.astype(F32)
        k32 = k.astype(F32)
        rq = lax.rsqrt(head_sum(q32 * q32, ones) * (1.0 / HD) + EPS)
        rk = lax.rsqrt(head_sum(k32 * k32, ones) * (1.0 / HD) + EPS)
        rq_s[chunk] = rq
        rk_s[chunk] = rk
        qn = (q32 * rq * gains[0:1, :]).astype(BF16)
        kn = (k32 * rk * gains[1:2, :]).astype(BF16)
        qn_s[chunk] = qn
        kn_s[chunk] = kn
        down = lax.broadcasted_iota(jnp.int32, (rows, rows), 0)
        along = lax.broadcasted_iota(jnp.int32, (rows, rows), 1)
        same = ((down ^ along) & (tokens - 1)) == 0
        attended = [None] * (PAD // LANES)
        for head in range(HEADS):
            scores = dot_nt(head_window(kn, head, True), head_window(qn, head, False)) * scale
            scores = jnp.where(same, scores, -1e30)
            shifted = jnp.exp(scores - jnp.max(scores, 0, keepdims=True))
            probs = shifted * (1.0 / jnp.sum(shifted, 0, keepdims=True))
            probs_s[chunk, head] = probs
            add_window(attended, head, dot_tn(probs.astype(BF16), head_window(v, head, True)))
        att_s[chunk] = jnp.concatenate(attended, axis=1).astype(BF16)
        return carry

    lax.fori_loop(0, chunks, forward, 0)

    def middle(chunk, carry):
        for i in range(nseq - 1):
            inward(1, chunk, i).wait()
        inward_own(1, chunk).wait()
        gated = (mod[2] * cot_tok[chunk].reshape(rows, width).astype(F32)).astype(BF16)
        ga = dot_nt(gated, out_w[...]).astype(BF16)
        ga_s[chunk] = jnp.concatenate([ga, jnp.zeros((rows, PAD - WIDE), BF16)], axis=1)
        share = dot_tn(att_s[chunk][:, 0:WIDE], gated)
        target = share_s if reduce_here else grad_w
        share = share.reshape(target.shape)

        @pl.when(chunk == 0)
        def _():
            target[...] = share

        @pl.when(chunk > 0)
        def _():
            target[...] += share

        return carry

    lax.fori_loop(0, chunks, middle, 0)

    chips = nseq // 2
    chip = lax.div(seq, 2)
    columns = width // ndp

    def to_pair():
        return pltpu.make_async_remote_copy(
            src_ref=pair_out,
            dst_ref=pair_in,
            send_sem=g_send.at[0],
            recv_sem=g_recv.at[0],
            device_id=to_core,
            device_id_type=MESH,
        )

    def to_chip(i):
        return pltpu.make_async_remote_copy(
            src_ref=far_out.at[i - 1],
            dst_ref=far_in.at[i - 1],
            send_sem=g_send.at[i],
            recv_sem=g_recv.at[i],
            device_id={"seq": lax.rem(chip + i, chips) * 2 + core},
            device_id_type=MESH,
        )

    def to_columns(i):
        return pltpu.make_async_remote_copy(
            src_ref=col_out.at[lax.rem(dp + i, ndp)],
            dst_ref=col_in.at[i - 1],
            send_sem=g_send.at[chips + i - 1],
            recv_sem=g_recv.at[chips + i - 1],
            device_id={"dp": lax.rem(dp + i, ndp)},
            device_id_type=MESH,
        )

    def reduce_chips():
        to_pair().wait()
        for i in range(1, chips):
            there = lax.rem(chip + i, chips)
            far_out[i - 1] = (share_s[there * 2 + core] + pair_in[there].astype(F32)).astype(BF16)
            to_chip(i).start()

    def reduce_columns():
        total = share_s[seq] + pair_in[chip].astype(F32)
        for i in range(1, chips):
            to_chip(i).wait()
            total = total + far_in[i - 1].astype(F32)
        for d in range(ndp):
            part = total[:, d * columns : (d + 1) * columns]
            col_out[d] = part.astype(BF16)

            @pl.when(dp == d)
            def _():
                grad_w[...] = part

        for i in range(1, ndp):
            to_columns(i).start()

    if reduce_here:
        for c in range(chips):
            pair_out[c] = share_s[2 * c + 1 - core].astype(BF16)
        to_pair().start()

    def backward(chunk, carry):
        qn = qn_s[chunk]
        kn = kn_s[chunk]
        v = v_s[chunk]
        ga = ga_s[chunk]
        grad_qn = [None] * (PAD // LANES)
        grad_kn = [None] * (PAD // LANES)
        grad_v = [None] * (PAD // LANES)
        for head in range(HEADS):
            probs = probs_s[chunk, head]
            ga_head = head_window(ga, head, True)
            grad_probs = dot_nt(head_window(v, head, False), ga_head)
            total = jnp.sum(probs * grad_probs, 0, keepdims=True)
            grad_scores = (probs * (grad_probs - total) * scale).astype(BF16)
            add_window(grad_v, head, dot_nn(probs.astype(BF16), ga_head))
            add_window(grad_qn, head, dot_tn(grad_scores, head_window(kn, head, True)))
            add_window(grad_kn, head, dot_nn(grad_scores, head_window(qn, head, True)))

        def through_norm(raw, inverse, gain, grads):
            raw = raw.astype(F32)
            scaled = jnp.concatenate(grads, axis=1) * gain
            mean = head_sum(raw * scaled, ones) * (1.0 / HD)
            return inverse * scaled - raw * inverse * inverse * inverse * mean

        grad_q = through_norm(q_s[chunk], rq_s[chunk], gains[0:1, :], grad_qn).astype(BF16)
        grad_k = pltpu.roll(
            through_norm(k_s[chunk], rk_s[chunk], gains[1:2, :], grad_kn), PAD - WIDE, 1
        ).astype(BF16)
        grad_v = jnp.concatenate(grad_v, axis=1)[:, 0:WIDE].astype(BF16)
        grad_mod = (
            dot_nt(grad_q, weights[:, 0:PAD])
            + dot_nt(grad_k, weights[:, k_low : k_low + PAD])
            + dot_nt(grad_v, weights[:, v_low : v_low + WIDE])
        ).astype(BF16)
        normed = normed_s[chunk]
        grad_normed = grad_mod.astype(F32) * (1.0 + mod[1])
        grad_ln = rinv_s[chunk] * (
            grad_normed
            - jnp.mean(grad_normed, -1, keepdims=True)
            - normed * jnp.mean(grad_normed * normed, -1, keepdims=True)
        )
        out = cot_tok[chunk].reshape(rows, width).astype(F32) + grad_ln
        gh_tok[chunk] = out.astype(BF16).reshape(frames, tokens, width)
        for i in range(nseq - 1):
            outward(chunk, i).start()
        outward_own(chunk).start()
        if reduce_here:

            @pl.when(chunk == 0)
            def _():
                reduce_chips()

            if chunks > 2:

                @pl.when(chunk == chunks - 2)
                def _():
                    reduce_columns()

        return carry

    lax.fori_loop(0, chunks, backward, 0)
    if reduce_here:
        if chunks <= 2:
            reduce_columns()
        for i in range(1, ndp):
            to_columns(i).wait()
            grad_w[...] += col_in[i - 1].astype(F32)
    if gather_here:
        for i in order:

            @pl.when(relays(i))
            def _():
                hand_on(1, i, group, to_group).wait_send()
                hand_on(2, i, group, to_core).wait_send()
                hand_on(3, i, 1 - group, to_core).wait_send()

        @pl.when(lax.rem(dp, 2) == core)
        def _():
            for i in range(1, ndp):
                along_dp(i).wait_send()

    for chunk in range(chunks):
        for i in range(nseq - 1):
            outward(chunk, i).wait()
        outward_own(chunk).wait()


def shards(nseq, ndp, hidden_states, modulation, qkv_weight, qk_gain, out_weight, out_cotangent):
    mine, all_tokens, width = hidden_states.shape[1:]
    frames = mine * nseq
    block = all_tokens // nseq
    tokens = min(block, max(16, 128 // frames))
    chunks = block // tokens
    rows = frames * tokens
    gather_here = qkv_weight.shape[0] % 32 == 0
    if not gather_here:
        qkv_weight = lax.all_gather(qkv_weight, "dp", axis=0, tiled=True)
    lane = np.arange(PAD)
    inside = (lane < WIDE)[:, None] & (lane[:, None] // HD == lane[None, :] // HD)
    ones = jnp.asarray(inside.astype(np.float32), BF16)
    out_rows = WIDE // nseq
    columns = width // ndp
    reduce_here = out_rows % 16 == 0
    sizes = (nseq, ndp, frames, chunks, tokens, width, gather_here, reduce_here)
    if reduce_here:
        share_shape = (out_rows, columns)
        share_scratch = [
            pltpu.VMEM((nseq, out_rows, width), F32),
            pltpu.VMEM((nseq // 2, out_rows, width), BF16),
            pltpu.VMEM((nseq // 2, out_rows, width), BF16),
            pltpu.VMEM((nseq // 2 - 1, out_rows, width), BF16),
            pltpu.VMEM((nseq // 2 - 1, out_rows, width), BF16),
            pltpu.VMEM((ndp, out_rows, columns), BF16),
            pltpu.VMEM((ndp - 1, out_rows, columns), BF16),
        ]
    else:
        share_shape = (WIDE, width)
        share_scratch = [pltpu.VMEM((16, LANES), F32)] * 7
    anywhere = pl.BlockSpec(memory_space=pl.ANY)
    vmem = pl.BlockSpec(memory_space=pltpu.VMEM)

    def wide(dtype):
        return pltpu.VMEM((chunks, rows, PAD), dtype)

    by_token = pltpu.VMEM((chunks, frames, tokens, width), BF16)
    grad_hidden, share = pl.pallas_call(
        functools.partial(kernel, sizes),
        out_shape=(
            jax.ShapeDtypeStruct((mine, all_tokens, width), BF16),
            jax.ShapeDtypeStruct(share_shape, F32),
        ),
        in_specs=[anywhere, anywhere, anywhere, vmem, vmem, vmem, vmem],
        out_specs=(anywhere, vmem),
        scratch_shapes=[
            by_token,
            by_token,
            by_token,
            pltpu.VMEM((width, 3 * WIDE), BF16),
            pltpu.VMEM((chunks, rows, width), F32),
            pltpu.VMEM((chunks, rows, width), BF16),
            pltpu.VMEM((chunks, rows, 1), F32),
            wide(BF16),
            wide(BF16),
            wide(BF16),
            wide(F32),
            wide(F32),
            wide(BF16),
            wide(BF16),
            wide(BF16),
            wide(BF16),
            pltpu.VMEM((chunks, HEADS, rows, rows), F32),
            pltpu.SemaphoreType.DMA((3, chunks, nseq - 1)),
            pltpu.SemaphoreType.DMA((3, chunks, nseq - 1)),
            pltpu.SemaphoreType.DMA((3, chunks)),
            pltpu.SemaphoreType.DMA((4, ndp)),
            pltpu.SemaphoreType.DMA((4, ndp)),
            pltpu.SemaphoreType.DMA,
            *share_scratch,
            pltpu.SemaphoreType.DMA((nseq // 2 + ndp,)),
            pltpu.SemaphoreType.DMA((nseq // 2 + ndp,)),
        ],
        compiler_params=pltpu.CompilerParams(
            collective_id=0, has_side_effects=True, vmem_limit_bytes=56 * 2**20
        ),
        cost_estimate=pl.CostEstimate(
            flops=12_000_000_000, bytes_accessed=20_000_000, transcendentals=2_000_000
        ),
    )(hidden_states[0], out_cotangent[0], qkv_weight, modulation.transpose(1, 0, 2), qk_gain, out_weight, ones)
    if not reduce_here:
        share = lax.psum_scatter(share, "seq", scatter_dimension=0, tiled=True)
        share = lax.psum_scatter(share, "dp", scatter_dimension=1, tiled=True)
    return (grad_hidden[None], share)


def solution(mesh):
    placed = (
        P(("groups", "dp"), "seq", None, None),
        P(("groups", "dp"), None, None),
        P("dp", None),
        P(),
        P(),
        P(("groups", "dp"), "seq", None, None),
    )
    return jax.shard_map(
        functools.partial(shards, mesh.shape["seq"], mesh.shape["dp"]),
        mesh=mesh,
        in_specs=placed,
        out_specs=(P(("groups", "dp"), "seq", None, None), P(("groups", "seq"), "dp")),
        check_vma=False,
    )
```
